32 devices in a mesh: groups: 2 (over y), sec: 4 (over z), row: 2 (over x), rep: 2 (over core).
Axes of the slice: x: 2, y: 2, z: 4, core: 2. Of those that a mesh axis runs over, the one named last changes fastest.
Arguments:
- psi: bfloat16 [128, 256, 256], P(('groups', 'sec')), parts along dimension 0, may hold values from -6 to 6
- left_environment_blocks: bfloat16 [16, 24, 256, 256], P(('groups', 'sec'), 'rep', 'row'), parts along dimension 0, may hold values from -0.078125 to 0.078125
- right_env: bfloat16 [16, 24, 256, 256], P(('groups', 'sec'), 'rep', 'row'), parts along dimension 0, may hold values from -0.375 to 0.375
- pair_dest: int32 [128, 1], P(('groups', 'sec')), parts along dimension 0, may hold values from 0 to 3; in each aligned block of 16 rows (0 to 15, 16 to 31, ...) at most 8 rows name the same one
- pair_left_sector: int32 [128], P(('groups', 'sec')), parts along dimension 0, may hold values from 0 to 1
- pair_right: int32 [128], P(('groups', 'sec')), parts along dimension 0, may hold values from 0 to 1
Outputs:
- mixed: bfloat16 [8, 32, 256, 256], P(('groups', 'sec'), 'rep', 'row'), parts along dimension 0
The draws below stay inside these ranges and needn't reach their ends.
There are 2 independent parts, one for each index of `groups`. The reference program is written for one: setup_inputs(seed, part) draws one part's arguments, and reference() takes and returns one part's arrays. A program takes and returns all parts, laid end to end along the dimension named above; each array names one. Nothing has to cross between parts.
Inputs may be any that keep to these rules, and one draw needn't show every extreme that they name: `pair_dest`: among the 16 pairs of one sec index no destination is named more than 8 times, a bound that some block reaches.
All inputs are finite; a program needn't handle non-finite values.
Results may differ from the reference program's by a relative error of at most 0.005.
Values may be sent and summed in bfloat16 or wider, within the bound.
A program may use at most 192 MiB of HBM per device.

```python
import math
import jax
import jax.numpy as jnp
import numpy as np
from jax import lax

BLOCK_WIDTH = 256
W = 24
SPD = 2
PD = 16
CAP = 8
OUTPUT_SLOTS = 32
NPAIR = 64
NSECTOR = 8
N_SEC = 4


def with_ends(drawn, stream_key, smallest, high):
    shape = drawn.shape
    index_at = [jax.random.randint(jax.random.fold_in(stream_key, axis), (), 0, shape[axis]) for axis in range(len(shape))]
    drawn = drawn.at[tuple(index_at)].set(smallest)
    longest = shape.index(max(shape))
    index_at[longest] = (index_at[longest] + 1) % shape[longest]
    return drawn.at[tuple(index_at)].set(high)


def shard_levels(own_key, extent, shards, least, top_value):
    def one(dim, parts):
        draws = jax.random.uniform(jax.random.fold_in(jax.random.fold_in(own_key, 6), dim), (parts,), jnp.float32, least / len(shards), top_value / len(shards))
        return jnp.repeat(jnp.exp(draws), extent[dim] // parts).reshape((-1,) + (1,) * (len(extent) - dim - 1))

    gain = one(*shards[0])
    for cut in shards[1:]:
        gain = gain * one(*cut)
    return gain


def deal_out(rng, own, number, rows, amount, top, most, lean):
    order = jax.random.permutation(rng, amount)
    packed, common = load_shares(amount, rows * top, most, lean, True), load_shares(amount, rows * top, most, lean, False)
    places = jnp.arange(amount)

    def named(sizes, turn):
        used = int((sizes > 0).sum())
        fixed = max(1, used // 4)
        moved = fixed + (places - fixed + turn * (used - fixed)) % max(1, amount - fixed)
        return jnp.zeros((amount,), jnp.int32).at[order[jnp.where(places < fixed, places, moved)]].set(jnp.asarray(sizes, jnp.int32))

    sizes = jnp.where(number % 4 == 0, named(packed, number // 4), named(common, number - number // 4 - 1))
    mixed = jax.random.permutation(jax.random.fold_in(own, 3), amount)
    source_of, receiver = mixed[0:amount // 2 * 2:2], mixed[1:amount // 2 * 2:2]
    margin = jnp.minimum(sizes[source_of] - 1, most - sizes[receiver]) // 2
    margin = jnp.where((source_of == order[0]) | (receiver == order[0]) | (sizes[receiver] == 0), 0, jnp.maximum(margin, 0))
    moved = jax.random.randint(jax.random.fold_in(own, 4), (amount // 2,), 0, 1 << 20) % (margin + 1)
    sizes = sizes.at[source_of].add(-moved).at[receiver].add(moved)
    labels = jnp.searchsorted(jnp.cumsum(sizes), jnp.arange(rows * top), side="right").astype(jnp.int32)
    listing = labels.reshape(top, rows).T
    listing = listing[jax.random.permutation(jax.random.fold_in(own, 1), rows)]
    turn = jax.random.randint(jax.random.fold_in(own, 2), (rows, 1), 0, top)
    return jnp.take_along_axis(listing, (jnp.arange(top)[None, :] + turn) % top, axis=1)


def load_shares(count, total, bound, skew, full):
    weights = [(1 << 20) // math.isqrt(standing ** skew) + 1 for standing in range(1, count + 1)]
    largest = bound if full else min(bound, max(-(-total // count), total * weights[0] // sum(weights)))
    least = 1 if total - largest >= count - 1 else 0
    counts, rest = [largest] + [least] * (count - 1), total - largest - least * (count - 1)
    while rest > 0:
        candidates = [i for i in range(1, count) if counts[i] < largest] or [i for i in range(1, count) if counts[i] < bound]
        whole, remaining = sum([weights[i] for i in candidates]), rest
        for i in candidates:
            extra = min(bound - counts[i], max(1, remaining * weights[i] // whole), rest)
            counts[i] = counts[i] + extra
            rest = rest - extra
    return np.array(counts)


def centred(own_key, shape, deviation, most, pieces=(), held_as=jnp.bfloat16):
    gain = shard_levels(own_key, shape, pieces, -0.22, 0.18) if pieces else 1.0
    entries = jax.random.normal(own_key, shape, jnp.float32) * deviation * gain
    return jnp.minimum(jnp.maximum(entries, -most), most).astype(held_as)


def setup_inputs(seed: int = 0, part: int = 0) -> dict:
    arg_keys = jax.random.split(jax.random.key(seed), 7)
    part_splits = jax.random.split(jax.random.fold_in(arg_keys[6], part), 7)
    psi = centred(part_splits[0], (NPAIR, BLOCK_WIDTH, BLOCK_WIDTH), 1.0, 6.0, ((0, 4),))
    left_environment_blocks = centred(part_splits[1], (NSECTOR, W, BLOCK_WIDTH, BLOCK_WIDTH), (BLOCK_WIDTH * W) ** -0.5, 0.078125, ((0, 4), (1, 2), (2, 2)))
    right_env = centred(part_splits[2], (NSECTOR, W, BLOCK_WIDTH, BLOCK_WIDTH), BLOCK_WIDTH ** -0.5, 0.375, ((0, 4), (1, 2), (2, 2)))
    pair_dest_keys = jax.random.split(jax.random.fold_in(part_splits[3], 1), NPAIR // PD)
    pair_dest_turns = jax.random.permutation(jax.random.fold_in(part_splits[3], 3), NPAIR // PD)
    pair_dest = jax.vmap(lambda own, number: deal_out(jax.random.fold_in(part_splits[3], 2), own, number, PD, N_SEC, 1, CAP, 2))(pair_dest_keys, pair_dest_turns).reshape((NPAIR, 1))
    pair_left_sector = with_ends(jax.random.randint(part_splits[4], (NPAIR,), 0, SPD), jax.random.fold_in(part_splits[4], 1), 0, SPD - 1).astype(jnp.int32)
    pair_right = with_ends(jax.random.randint(part_splits[5], (NPAIR,), 0, SPD), jax.random.fold_in(part_splits[5], 1), 0, SPD - 1).astype(jnp.int32)
    return dict(psi=psi, left_environment_blocks=left_environment_blocks, right_env=right_env, pair_dest=pair_dest, pair_left_sector=pair_left_sector, pair_right=pair_right)


def reference(psi, left_environment_blocks, right_env, pair_dest, pair_left_sector, pair_right):
    targets = pair_dest[:, 0]
    source_sec = (jnp.arange(NPAIR) // PD).astype(jnp.int32)
    grid_dest = targets.reshape(N_SEC, PD)
    grid_hot = (grid_dest[:, :, None] == jnp.arange(N_SEC)[None, None, :]).astype(jnp.int32)
    previous_step = jnp.cumsum(grid_hot, axis=1) - grid_hot
    ranking = jnp.sum(grid_hot * previous_step, axis=-1).reshape(NPAIR).astype(jnp.int32)
    left_sector = (source_sec * SPD + pair_left_sector).astype(jnp.int32)
    right_sector = (targets * SPD + pair_right).astype(jnp.int32)

    def one_pair(items):
        block, left_position, right_index = items
        left_blocks = left_environment_blocks[left_position].astype(jnp.float32)
        product = jnp.einsum("wab,bc->wac", left_blocks, block.astype(jnp.float32))
        product = lax.optimization_barrier(product.astype(jnp.bfloat16)).astype(jnp.float32)
        right_blocks = right_env[right_index].astype(jnp.float32)
        return jnp.einsum("wab,wbc->ac", product, right_blocks).astype(jnp.bfloat16)

    results = lax.map(one_pair, (psi, left_sector, right_sector))
    slot_index = (source_sec * CAP + ranking).astype(jnp.int32)
    mixed = jnp.zeros((N_SEC, OUTPUT_SLOTS, BLOCK_WIDTH, BLOCK_WIDTH), jnp.bfloat16)
    return mixed.at[targets, slot_index].set(results)
```

```python
import functools

import jax
import jax.numpy as jnp
from jax import lax
from jax.experimental import pallas as pl
from jax.experimental.pallas import tpu as pltpu
from jax.sharding import PartitionSpec as P

MESH = pl.DeviceIdType.MESH


def remote(src, dst, send, recv, where):
    return pltpu.make_async_remote_copy(
        src_ref=src, dst_ref=dst, send_sem=send, recv_sem=recv, device_id=where, device_id_type=MESH
    )


def kernel(
    sizes,
    fill_ref,
    left_ref,
    right_ref,
    psi_ref,
    lenv_ref,
    renv_ref,
    out_ref,
    stage,
    psi_in,
    lfar,
    rfull,
    acc,
    peer,
    psi_send,
    psi_recv,
    row_send,
    row_recv,
    rep_send,
    rep_recv,
    rrow_send,
    rrow_recv,
    up_send,
    down_send,
    l_recv,
    sum_send,
    sum_recv,
):
    secs, rows, capacity, chunks = sizes
    bonds, height, width = lenv_ref.shape[1:]
    step = bonds // chunks
    part = width // (2 * rows)
    half = secs // 2
    me = lax.axis_index("sec")
    row = lax.axis_index("row")
    rep = lax.axis_index("rep")
    other = 1 - rep
    mine = row * 2 + rep

    def bars(q):
        return pl.ds(pl.multiple_of(q * part, part), part)

    barrier = pltpu.get_barrier_semaphore()
    for h in range(1, secs):
        pl.semaphore_signal(
            barrier, inc=1, device_id={"sec": lax.rem(me + h, secs)}, device_id_type=MESH
        )
    for h in range(1, rows):
        pl.semaphore_signal(
            barrier, inc=1, device_id={"row": lax.rem(row + h, rows)}, device_id_type=MESH
        )
    pl.semaphore_signal(barrier, inc=1, device_id={"rep": other}, device_id_type=MESH)
    pl.semaphore_wait(barrier, secs + rows - 1)

    def l_copy(source, c, src, direction):
        sends = up_send if direction == 1 else down_send
        return remote(
            src,
            lfar.at[source, c],
            sends.at[source, c],
            l_recv.at[source, c],
            {"sec": me + direction},
        )

    def chunk_of(c):
        return lenv_ref.at[:, pl.ds(c * step, step)]

    def fill(d):
        for j in range(capacity):
            p = fill_ref[d * capacity + j]
            block = psi_ref[jnp.maximum(p, 0), bars(mine), :]
            stage[d, j] = jnp.where(p >= 0, block, jnp.zeros_like(block))

    def psi_copy(d, source):
        return remote(
            stage.at[d],
            psi_in.at[source, mine],
            psi_send.at[d],
            psi_recv.at[source],
            {"sec": d},
        )

    for h in range(1, secs):
        d = lax.rem(me + h, secs)
        fill(d)
        psi_copy(d, me).start()

    for c in range(chunks):

        @pl.when(me + 1 < secs)
        def _():
            l_copy(me, c, chunk_of(c), 1).start()

        @pl.when(me > 0)
        def _():
            l_copy(me, c, chunk_of(c), -1).start()

    def r_copy(h, owner):
        return remote(
            renv_ref,
            rfull.at[owner],
            rrow_send.at[h],
            rrow_recv.at[owner],
            {"row": lax.rem(row + h, rows)},
        )

    for h in range(1, rows):
        r_copy(h, row).start()
    rfull[row] = renv_ref[...]

    for j in range(capacity):
        p = fill_ref[me * capacity + j]
        for q in range(2 * rows):
            block = psi_ref[jnp.maximum(p, 0), pl.ds(q * part, part), :]
            psi_in[me, q, j] = jnp.where(p >= 0, block, jnp.zeros_like(block))

    def row_copy(source, h, to):
        return remote(
            psi_in.at[source, mine],
            psi_in.at[source, mine],
            row_send.at[source, h],
            row_recv.at[source, row],
            {"row": to},
        )

    def rep_copy(source, r):
        bar = r * 2 + rep
        return remote(
            psi_in.at[source, bar],
            psi_in.at[source, bar],
            rep_send.at[source, r],
            rep_recv.at[source, r],
            {"rep": other},
        )

    for h in range(1, secs):
        source = lax.rem(me + secs - h, secs)
        psi_copy(source, source).wait_recv()
        for k in range(1, rows):
            row_copy(source, k, lax.rem(row + k, rows)).start()
        rep_copy(source, row).start()

    for h in range(1, rows):
        owner = lax.rem(row + h, rows)
        r_copy(h, owner).wait_recv()

    for h in range(1, secs):
        source = lax.rem(me + secs - h, secs)
        for k in range(1, rows):
            owner = lax.rem(row + k, rows)
            bar = owner * 2 + rep
            remote(
                psi_in.at[source, bar],
                psi_in.at[source, bar],
                row_send.at[source, k],
                row_recv.at[source, owner],
                {"row": owner},
            ).wait_recv()
            rep_copy(source, owner).start()

    for h in range(1, secs):
        source = lax.rem(me + secs - h, secs)
        for r in range(rows):
            rep_copy(source, r).wait_recv()

    def work(source, c, block):
        def one(j, carry):
            at = source * capacity + j
            ls = left_ref[at]
            rs = right_ref[at]
            low, high = block(0), block(1)
            a = jnp.where(ls == 0, low, high).reshape(step * height, width)
            x = psi_in[source, :, j].reshape(width, width)
            product = jnp.dot(a, x, preferred_element_type=jnp.float32).astype(jnp.bfloat16)
            total = None
            for w in range(step):
                b = rfull[:, rs, c * step + w].reshape(width, width)
                term = jnp.dot(
                    product[w * height : (w + 1) * height], b, preferred_element_type=jnp.float32
                )
                total = term if total is None else total + term
            if c == 0:
                acc[source, j] = total
            else:
                acc[source, j] += total
            return carry

        lax.fori_loop(0, capacity, one, 0)

    def sum_copy(source):
        return remote(
            acc.at[source],
            peer.at[lax.rem(source, half)],
            sum_send.at[source],
            sum_recv.at[lax.rem(source, half)],
            {"rep": other},
        )

    def hand_over(source):
        @pl.when(source // half != rep)
        def _():
            sum_copy(source).start()

    for c in range(chunks):
        work(me, c, lambda s: lenv_ref[s, pl.ds(c * step, step)])
    hand_over(me)

    for h in range(1, secs):
        for c in range(chunks):

            @pl.when(me >= h)
            def _():
                source = me - h
                l_copy(source, c, lfar.at[source, c], 1).wait_recv()

                @pl.when(me + 1 < secs)
                def _():
                    l_copy(source, c, lfar.at[source, c], 1).start()

            @pl.when(me + h < secs)
            def _():
                source = me + h
                l_copy(source, c, lfar.at[source, c], -1).wait_recv()

                @pl.when(me > 0)
                def _():
                    l_copy(source, c, lfar.at[source, c], -1).start()

            @pl.when(me >= h)
            def _():
                source = me - h
                work(source, c, lambda s: lfar[source, c, s])
                if c == chunks - 1:
                    hand_over(source)

            @pl.when(me + h < secs)
            def _():
                source = me + h
                work(source, c, lambda s: lfar[source, c, s])
                if c == chunks - 1:
                    hand_over(source)

    def finish(i, carry):
        source = rep * half + i
        sum_copy(source).wait_recv()

        def one(j, carry):
            out_ref[i * capacity + j] = (acc[source, j] + peer[i, j]).astype(out_ref.dtype)
            return carry

        return lax.fori_loop(0, capacity, one, carry)

    lax.fori_loop(0, half, finish, 0)

    for h in range(1, secs):
        d = lax.rem(me + h, secs)
        psi_copy(d, me).wait_send()
        for k in range(1, rows):
            row_copy(d, k, lax.rem(row + k, rows)).wait_send()
        for r in range(rows):
            rep_copy(d, r).wait_send()
    for h in range(1, rows):
        r_copy(h, row).wait_send()
    for c in range(chunks):
        for h in range(secs):

            @pl.when((me >= h) & (me + 1 < secs))
            def _():
                l_copy(me - h, c, lfar.at[me - h, c], 1).wait_send()

            @pl.when((me + h < secs) & (me > 0))
            def _():
                l_copy(me + h, c, lfar.at[me + h, c], -1).wait_send()

    def left(i, carry):
        sum_copy(other * half + i).wait_send()
        return carry

    lax.fori_loop(0, half, left, 0)


def body(rows, psi, left_environment_blocks, right_env, pair_dest, pair_left_sector, pair_right):
    secs = lax.axis_size("sec")
    me = lax.axis_index("sec")
    pairs = psi.shape[0]
    capacity = 2 * pairs // secs
    sectors, bonds, height, width = left_environment_blocks.shape
    chunks = 4
    step = bonds // chunks
    part = width // (2 * rows)
    code = pair_dest[:, 0] * 4 + pair_left_sector * 2 + pair_right
    codes = lax.all_gather(code, "sec", axis=0, tiled=True).reshape(secs, pairs)
    places = jnp.arange(pairs)
    slots = jnp.arange(capacity)

    def ranks(dest):
        same = dest[..., :, None] == dest[..., None, :]
        earlier = places[None, :] < places[:, None]
        return jnp.sum((same & earlier).astype(jnp.int32), axis=-1)

    targets = pair_dest[:, 0]
    match = (targets[None, None, :] == jnp.arange(secs)[:, None, None]) & (
        ranks(targets)[None, None, :] == slots[None, :, None]
    )
    fill = (jnp.sum(match.astype(jnp.int32) * (places + 1), axis=-1) - 1).reshape(-1)
    dest = codes // 4
    found = ((dest == me)[:, None, :] & (ranks(dest)[:, None, :] == slots[None, :, None])).astype(
        jnp.int32
    )
    at = jnp.sum(found * (codes % 4)[:, None, :], axis=-1).reshape(-1)
    bf16, f32 = jnp.bfloat16, jnp.float32
    dma = pltpu.SemaphoreType.DMA
    vmem = pl.BlockSpec(memory_space=pltpu.VMEM)
    smem = pl.BlockSpec(memory_space=pltpu.SMEM)
    out = pl.pallas_call(
        functools.partial(kernel, (secs, rows, capacity, chunks)),
        out_shape=jax.ShapeDtypeStruct((capacity * secs // 2, height, width), bf16),
        in_specs=[smem, smem, smem, vmem, vmem, vmem],
        out_specs=vmem,
        scratch_shapes=[
            pltpu.VMEM((secs, capacity, part, width), bf16),
            pltpu.VMEM((secs, 2 * rows, capacity, part, width), bf16),
            pltpu.VMEM((secs, chunks, sectors, step, height, width), bf16),
            pltpu.VMEM((rows, sectors, bonds, height, width), bf16),
            pltpu.VMEM((secs, capacity, height, width), f32),
            pltpu.VMEM((secs // 2, capacity, height, width), f32),
            dma((secs,)),
            dma((secs,)),
            dma((secs, rows)),
            dma((secs, rows)),
            dma((secs, rows)),
            dma((secs, rows)),
            dma((rows,)),
            dma((rows,)),
            dma((secs, chunks)),
            dma((secs, chunks)),
            dma((secs, chunks)),
            dma((secs // 2 * 2,)),
            dma((secs // 2,)),
        ],
        compiler_params=pltpu.CompilerParams(
            collective_id=0, has_side_effects=True, vmem_limit_bytes=56 * 1024 * 1024
        ),
        cost_estimate=pl.CostEstimate(
            flops=4 * secs * capacity * bonds * height * width * width,
            bytes_accessed=8 * 1024 * 1024,
            transcendentals=0,
        ),
    )(fill, at // 2, at % 2, psi, left_environment_blocks, right_env)
    return out[None]


def solution(mesh):
    placed = (
        P(("groups", "sec"), None, None),
        P(("groups", "sec"), "rep", "row", None),
        P(("groups", "sec"), "rep", "row", None),
        P(("groups", "sec"), None),
        P(("groups", "sec")),
        P(("groups", "sec")),
    )
    return jax.shard_map(
        functools.partial(body, mesh.shape["row"]),
        mesh=mesh,
        in_specs=placed,
        out_specs=P(("groups", "sec"), "rep", "row", None),
        check_vma=False,
    )
```

```python
import functools

import jax
import jax.numpy as jnp
from jax import lax
from jax.experimental import pallas as pl
from jax.experimental.pallas import tpu as pltpu
from jax.sharding import PartitionSpec as P

MESH = pl.DeviceIdType.MESH


def remote(src, dst, send, recv, where):
    return pltpu.make_async_remote_copy(
        src_ref=src, dst_ref=dst, send_sem=send, recv_sem=recv, device_id=where, device_id_type=MESH
    )


def kernel(
    sizes,
    fill_ref,
    meta_ref,
    psi_ref,
    lenv_ref,
    renv_ref,
    out_ref,
    meta_far,
    codes,
    stage,
    psi_in,
    lfar,
    rfull,
    acc,
    peer,
    meta_send,
    meta_recv,
    code_sem,
    psi_send,
    psi_recv,
    row_send,
    row_recv,
    rep_send,
    rep_recv,
    rrow_send,
    rrow_recv,
    up_send,
    down_send,
    l_recv,
    sum_send,
    sum_recv,
):
    secs, rows, capacity, chunks = sizes
    bonds, height, width = lenv_ref.shape[1:]
    step = bonds // chunks
    part = width // (2 * rows)
    half = secs // 2
    unroll = 4 if capacity % 4 == 0 else capacity
    me = lax.axis_index("sec")
    row = lax.axis_index("row")
    rep = lax.axis_index("rep")
    other = 1 - rep
    mine = row * 2 + rep

    def bars(q):
        return pl.ds(pl.multiple_of(q * part, part), part)

    barrier = pltpu.get_barrier_semaphore()
    for h in range(1, secs):
        pl.semaphore_signal(
            barrier, inc=1, device_id={"sec": lax.rem(me + h, secs)}, device_id_type=MESH
        )
    for h in range(1, rows):
        pl.semaphore_signal(
            barrier, inc=1, device_id={"row": lax.rem(row + h, rows)}, device_id_type=MESH
        )
    pl.semaphore_signal(barrier, inc=1, device_id={"rep": other}, device_id_type=MESH)
    pl.semaphore_wait(barrier, secs + rows - 1)

    def l_copy(source, c, src, direction):
        sends = up_send if direction == 1 else down_send
        return remote(
            src,
            lfar.at[source, c],
            sends.at[source, c],
            l_recv.at[source, c],
            {"sec": me + direction},
        )

    def chunk_of(c):
        return lenv_ref.at[:, pl.ds(c * step, step)]

    def fill(d):
        for j in range(capacity):
            p = lax.shift_right_arithmetic(fill_ref[d, 0, j], 2) - 1
            block = psi_ref[jnp.maximum(p, 0), bars(mine), :]
            stage[d, j] = jnp.where(p >= 0, block, jnp.zeros_like(block))

    def psi_copy(d, source):
        return remote(
            stage.at[d],
            psi_in.at[source, mine],
            psi_send.at[d],
            psi_recv.at[source],
            {"sec": d},
        )

    def meta_copy(d, source):
        return remote(
            meta_ref.at[d],
            meta_far.at[source],
            meta_send.at[d],
            meta_recv.at[source],
            {"sec": d},
        )

    def code_copy(source, src):
        return pltpu.make_async_copy(src.at[source], codes.at[source], code_sem.at[source])

    for h in range(1, secs):
        d = lax.rem(me + h, secs)
        meta_copy(d, me).start()
        fill(d)
        psi_copy(d, me).start()
    code_copy(me, meta_ref).start()

    for c in range(chunks):

        @pl.when(me + 1 < secs)
        def _():
            l_copy(me, c, chunk_of(c), 1).start()

        @pl.when(me > 0)
        def _():
            l_copy(me, c, chunk_of(c), -1).start()

    def strip(owner):
        return pl.ds(pl.multiple_of(owner * height, height), height)

    def r_copy(h, owner):
        return remote(
            renv_ref,
            rfull.at[:, :, strip(owner)],
            rrow_send.at[h],
            rrow_recv.at[owner],
            {"row": lax.rem(row + h, rows)},
        )

    for h in range(1, rows):
        r_copy(h, row).start()
    rfull[:, :, strip(row)] = renv_ref[...]

    for j in range(capacity):
        p = lax.shift_right_arithmetic(fill_ref[me, 0, j], 2) - 1
        for q in range(2 * rows):
            block = psi_ref[jnp.maximum(p, 0), pl.ds(q * part, part), :]
            psi_in[me, q, j] = jnp.where(p >= 0, block, jnp.zeros_like(block))

    def row_copy(source, h, to):
        return remote(
            psi_in.at[source, mine],
            psi_in.at[source, mine],
            row_send.at[source, h],
            row_recv.at[source, row],
            {"row": to},
        )

    def rep_copy(source, r):
        bar = r * 2 + rep
        return remote(
            psi_in.at[source, bar],
            psi_in.at[source, bar],
            rep_send.at[source, r],
            rep_recv.at[source, r],
            {"rep": other},
        )

    for h in range(1, secs):
        source = lax.rem(me + secs - h, secs)
        meta_copy(source, source).wait_recv()
        code_copy(source, meta_far).start()
        psi_copy(source, source).wait_recv()
        for k in range(1, rows):
            row_copy(source, k, lax.rem(row + k, rows)).start()
        rep_copy(source, row).start()

    for h in range(1, rows):
        owner = lax.rem(row + h, rows)
        r_copy(h, owner).wait_recv()

    for h in range(1, secs):
        source = lax.rem(me + secs - h, secs)
        for k in range(1, rows):
            owner = lax.rem(row + k, rows)
            bar = owner * 2 + rep
            remote(
                psi_in.at[source, bar],
                psi_in.at[source, bar],
                row_send.at[source, k],
                row_recv.at[source, owner],
                {"row": owner},
            ).wait_recv()
            rep_copy(source, owner).start()

    def work(source, c, block):
        def one(j, carry):
            code = codes[source, 0, j]
            ls = lax.rem(lax.shift_right_arithmetic(code, 1), 2)
            rs = lax.rem(code, 2)
            a = jnp.where(ls == 0, block(0), block(1)).reshape(step * height, width)
            x = psi_in[source, :, j].reshape(width, width)
            product = jnp.dot(a, x, preferred_element_type=jnp.float32).astype(jnp.bfloat16)
            wide = jnp.concatenate(
                [product[w * height : (w + 1) * height] for w in range(step)], axis=1
            )
            b = rfull[rs, pl.ds(c * step, step)].reshape(step * width, width)
            total = jnp.dot(wide, b, preferred_element_type=jnp.float32)
            if c == 0:
                acc[source, j] = total
            else:
                acc[source, j] += total
            return carry

        lax.fori_loop(0, capacity, one, 0, unroll=unroll)

    def sum_copy(source):
        return remote(
            acc.at[source],
            peer.at[lax.rem(source, half)],
            sum_send.at[source],
            sum_recv.at[lax.rem(source, half)],
            {"rep": other},
        )

    def hand_over(source):
        @pl.when(source // half != rep)
        def _():
            sum_copy(source).start()

    for h in range(secs):
        code_copy(lax.rem(me + h, secs), meta_ref).wait()
    for c in range(chunks):
        work(me, c, lambda s: lenv_ref[s, pl.ds(c * step, step)])
    hand_over(me)

    for h in range(1, secs):
        source = lax.rem(me + secs - h, secs)
        for r in range(rows):
            rep_copy(source, r).wait_recv()

    for h in range(1, secs):
        for c in range(chunks):

            @pl.when(me >= h)
            def _():
                source = me - h
                l_copy(source, c, lfar.at[source, c], 1).wait_recv()

                @pl.when(me + 1 < secs)
                def _():
                    l_copy(source, c, lfar.at[source, c], 1).start()

            @pl.when(me + h < secs)
            def _():
                source = me + h
                l_copy(source, c, lfar.at[source, c], -1).wait_recv()

                @pl.when(me > 0)
                def _():
                    l_copy(source, c, lfar.at[source, c], -1).start()

            @pl.when(me >= h)
            def _():
                source = me - h
                work(source, c, lambda s: lfar[source, c, s])
                if c == chunks - 1:
                    hand_over(source)

            @pl.when(me + h < secs)
            def _():
                source = me + h
                work(source, c, lambda s: lfar[source, c, s])
                if c == chunks - 1:
                    hand_over(source)

    def finish(i, carry):
        source = rep * half + i
        sum_copy(source).wait_recv()

        def one(j, carry):
            out_ref[i * capacity + j] = (acc[source, j] + peer[i, j]).astype(out_ref.dtype)
            return carry

        return lax.fori_loop(0, capacity, one, carry)

    lax.fori_loop(0, half, finish, 0)

    for h in range(1, secs):
        d = lax.rem(me + h, secs)
        meta_copy(d, me).wait_send()
        psi_copy(d, me).wait_send()
        for k in range(1, rows):
            row_copy(d, k, lax.rem(row + k, rows)).wait_send()
        for r in range(rows):
            rep_copy(d, r).wait_send()
    for h in range(1, rows):
        r_copy(h, row).wait_send()
    for c in range(chunks):
        for h in range(secs):

            @pl.when((me >= h) & (me + 1 < secs))
            def _():
                l_copy(me - h, c, lfar.at[me - h, c], 1).wait_send()

            @pl.when((me + h < secs) & (me > 0))
            def _():
                l_copy(me + h, c, lfar.at[me + h, c], -1).wait_send()

    def left(i, carry):
        sum_copy(other * half + i).wait_send()
        return carry

    lax.fori_loop(0, half, left, 0)


def body(rows, psi, left_environment_blocks, right_env, pair_dest, pair_left_sector, pair_right):
    secs = lax.axis_size("sec")
    pairs = psi.shape[0]
    capacity = 2 * pairs // secs
    sectors, bonds, height, width = left_environment_blocks.shape
    chunks = 4
    step = bonds // chunks
    part = width // (2 * rows)
    targets = pair_dest[:, 0]
    places = jnp.arange(pairs)
    same = targets[:, None] == targets[None, :]
    rank = jnp.sum((same & (places[None, :] < places[:, None])).astype(jnp.int32), axis=-1)
    value = (places + 1) * 4 + pair_left_sector * 2 + pair_right
    match = (targets[None, :] == jnp.arange(secs)[:, None])[:, None, :] & (
        rank[None, :] == jnp.arange(128)[:, None]
    )[None]
    meta = jnp.sum(jnp.where(match, value, 0), axis=-1)[:, None, :]
    bf16, f32 = jnp.bfloat16, jnp.float32
    dma = pltpu.SemaphoreType.DMA
    vmem = pl.BlockSpec(memory_space=pltpu.VMEM)
    smem = pl.BlockSpec(memory_space=pltpu.SMEM)
    out = pl.pallas_call(
        functools.partial(kernel, (secs, rows, capacity, chunks)),
        out_shape=jax.ShapeDtypeStruct((capacity * secs // 2, height, width), bf16),
        in_specs=[smem, vmem, vmem, vmem, vmem],
        out_specs=vmem,
        scratch_shapes=[
            pltpu.VMEM((secs, 1, 128), jnp.int32),
            pltpu.SMEM((secs, 1, 128), jnp.int32),
            pltpu.VMEM((secs, capacity, part, width), bf16),
            pltpu.VMEM((secs, 2 * rows, capacity, part, width), bf16),
            pltpu.VMEM((secs, chunks, sectors, step, height, width), bf16),
            pltpu.VMEM((sectors, bonds, rows * height, width), bf16),
            pltpu.VMEM((secs, capacity, height, width), f32),
            pltpu.VMEM((secs // 2, capacity, height, width), f32),
            dma((secs,)),
            dma((secs,)),
            dma((secs,)),
            dma((secs,)),
            dma((secs,)),
            dma((secs, rows)),
            dma((secs, rows)),
            dma((secs, rows)),
            dma((secs, rows)),
            dma((rows,)),
            dma((rows,)),
            dma((secs, chunks)),
            dma((secs, chunks)),
            dma((secs, chunks)),
            dma((secs // 2 * 2,)),
            dma((secs // 2,)),
        ],
        compiler_params=pltpu.CompilerParams(
            collective_id=0, has_side_effects=True, vmem_limit_bytes=56 * 1024 * 1024
        ),
        cost_estimate=pl.CostEstimate(
            flops=4 * secs * capacity * bonds * height * width * width,
            bytes_accessed=8 * 1024 * 1024,
            transcendentals=0,
        ),
    )(meta, meta, psi, left_environment_blocks, right_env)
    return out[None]


def solution(mesh):
    placed = (
        P(("groups", "sec"), None, None),
        P(("groups", "sec"), "rep", "row", None),
        P(("groups", "sec"), "rep", "row", None),
        P(("groups", "sec"), None),
        P(("groups", "sec")),
        P(("groups", "sec")),
    )
    return jax.shard_map(
        functools.partial(body, mesh.shape["row"]),
        mesh=mesh,
        in_specs=placed,
        out_specs=P(("groups", "sec"), "rep", "row", None),
        check_vma=False,
    )
```

```python
import functools

import jax
import jax.numpy as jnp
from jax import lax
from jax.experimental import pallas as pl
from jax.experimental.pallas import tpu as pltpu
from jax.sharding import PartitionSpec as P

MESH = pl.DeviceIdType.MESH


def remote(src, dst, send, recv, where):
    return pltpu.make_async_remote_copy(
        src_ref=src, dst_ref=dst, send_sem=send, recv_sem=recv, device_id=where, device_id_type=MESH
    )


def kernel(
    sizes,
    fill_ref,
    meta_ref,
    psi_ref,
    lenv_ref,
    renv_ref,
    out_ref,
    meta_far,
    codes,
    stage,
    psi_in,
    lfar,
    rfull,
    acc,
    peer,
    rhelp,
    ready,
    land,
    rh_send,
    rh_recv,
    rhrow_send,
    rhrow_recv,
    out_send,
    out_recv,
    meta_send,
    meta_recv,
    code_sem,
    psi_send,
    psi_recv,
    row_send,
    row_recv,
    rep_send,
    rep_recv,
    rrow_send,
    rrow_recv,
    up_send,
    down_send,
    l_recv,
    sum_send,
    sum_recv,
):
    secs, rows, capacity, chunks = sizes
    bonds, height, width = lenv_ref.shape[1:]
    step = bonds // chunks
    part = width // (2 * rows)
    half = secs // 2
    unroll = 4 if capacity % 4 == 0 else capacity
    me = lax.axis_index("sec")
    row = lax.axis_index("row")
    rep = lax.axis_index("rep")
    other = 1 - rep
    mine = row * 2 + rep
    last = secs - 1
    is_end = (me == 0) | (me == last)
    helper = (me == 1) | (me == last - 1)
    end = lax.div(me - 1, secs - 3) * last
    opposite = last - end
    aide = 1 + lax.div(me, last) * (secs - 3)

    def near(a):
        return (me + a != last) | ((me != 0) & (me != last))

    def far(a):
        return (me + a == last) & is_end

    def bars(q):
        return pl.ds(pl.multiple_of(q * part, part), part)

    barrier = pltpu.get_barrier_semaphore()
    for h in range(1, secs):
        pl.semaphore_signal(
            barrier, inc=1, device_id={"sec": lax.rem(me + h, secs)}, device_id_type=MESH
        )
    for h in range(1, rows):
        pl.semaphore_signal(
            barrier, inc=1, device_id={"row": lax.rem(row + h, rows)}, device_id_type=MESH
        )
    pl.semaphore_signal(barrier, inc=1, device_id={"rep": other}, device_id_type=MESH)
    pl.semaphore_wait(barrier, secs + rows - 1)

    def l_copy(source, c, src, direction):
        sends = up_send if direction == 1 else down_send
        return remote(
            src,
            lfar.at[source, c],
            sends.at[source, c],
            l_recv.at[source, c],
            {"sec": me + direction},
        )

    def chunk_of(c):
        return lenv_ref.at[:, pl.ds(c * step, step)]

    def strip(owner):
        return pl.ds(pl.multiple_of(owner * height, height), height)

    def help_copy(c):
        return remote(
            renv_ref.at[:, pl.ds(c * step, step)],
            rhelp.at[:, pl.ds(c * step, step), strip(row)],
            rh_send.at[c],
            rh_recv.at[c],
            {"sec": aide},
        )

    def help_row(c, h, owner):
        block = rhelp.at[:, pl.ds(c * step, step), strip(owner)]
        return remote(
            block,
            block,
            rhrow_send.at[c, h],
            rhrow_recv.at[c, owner],
            {"row": lax.rem(row + h, rows)},
        )

    def fill(d):
        for j in range(capacity):
            p = lax.shift_right_arithmetic(fill_ref[d, 0, j], 2) - 1
            block = psi_ref[jnp.maximum(p, 0), bars(mine), :]
            stage[d, j] = jnp.where(p >= 0, block, jnp.zeros_like(block))

    def psi_copy(d, source):
        return remote(
            stage.at[d],
            psi_in.at[source, mine],
            psi_send.at[d],
            psi_recv.at[source],
            {"sec": d},
        )

    def meta_copy(d, source):
        return remote(
            meta_ref.at[d],
            meta_far.at[source],
            meta_send.at[d],
            meta_recv.at[source],
            {"sec": d},
        )

    def code_copy(source, src):
        return pltpu.make_async_copy(src.at[source], codes.at[source], code_sem.at[source])

    for h in range(1, secs):
        d = lax.rem(me + h, secs)
        fill(d)

        @pl.when(near(d))
        def _():
            meta_copy(d, me).start()
            psi_copy(d, me).start()

        @pl.when(far(d))
        def _():
            to = 1 + lax.div(d, last) * (secs - 3)
            remote(
                meta_ref.at[d], meta_far.at[secs], meta_send.at[d], meta_recv.at[secs], {"sec": to}
            ).start()
            remote(
                stage.at[d],
                psi_in.at[secs, mine],
                psi_send.at[d],
                psi_recv.at[secs],
                {"sec": to},
            ).start()

    code_copy(me, meta_ref).start()

    for c in range(chunks):

        @pl.when(me + 1 < secs)
        def _():
            l_copy(me, c, chunk_of(c), 1).start()

        @pl.when(me > 0)
        def _():
            l_copy(me, c, chunk_of(c), -1).start()

        @pl.when(is_end)
        def _():
            help_copy(c).start()

    def r_copy(h, owner):
        return remote(
            renv_ref,
            rfull.at[:, :, strip(owner)],
            rrow_send.at[h],
            rrow_recv.at[owner],
            {"row": lax.rem(row + h, rows)},
        )

    for h in range(1, rows):
        r_copy(h, row).start()
    rfull[:, :, strip(row)] = renv_ref[...]

    for j in range(capacity):
        p = lax.shift_right_arithmetic(fill_ref[me, 0, j], 2) - 1
        for q in range(2 * rows):
            block = psi_ref[jnp.maximum(p, 0), pl.ds(q * part, part), :]
            psi_in[me, q, j] = jnp.where(p >= 0, block, jnp.zeros_like(block))

    def row_copy(source, h, to):
        return remote(
            psi_in.at[source, mine],
            psi_in.at[source, mine],
            row_send.at[source, h],
            row_recv.at[source, row],
            {"row": to},
        )

    def rep_copy(source, r):
        bar = r * 2 + rep
        return remote(
            psi_in.at[source, bar],
            psi_in.at[source, bar],
            rep_send.at[source, r],
            rep_recv.at[source, r],
            {"rep": other},
        )

    def arrived(source, at):
        meta_copy(me, at).wait_recv()
        code_copy(at, meta_far).start()
        psi_copy(me, at).wait_recv()
        for k in range(1, rows):
            row_copy(at, k, lax.rem(row + k, rows)).start()
        rep_copy(at, row).start()

    def spread(at):
        for k in range(1, rows):
            owner = lax.rem(row + k, rows)
            bar = owner * 2 + rep
            remote(
                psi_in.at[at, bar],
                psi_in.at[at, bar],
                row_send.at[at, k],
                row_recv.at[at, owner],
                {"row": owner},
            ).wait_recv()
            rep_copy(at, owner).start()

    def spread_done(at):
        for r in range(rows):
            rep_copy(at, r).wait_recv()

    def spread_left(at):
        for k in range(1, rows):
            row_copy(at, k, lax.rem(row + k, rows)).wait_send()
        for r in range(rows):
            rep_copy(at, r).wait_send()

    def each(action):
        for h in range(1, secs):
            source = lax.rem(me + secs - h, secs)

            @pl.when(near(source))
            def _():
                action(source)

        @pl.when(helper)
        def _():
            action(secs)

    each(lambda at: arrived(at, at))
    for h in range(1, rows):
        r_copy(h, lax.rem(row + h, rows)).wait_recv()
    each(spread)

    def work(source, c, block, right):
        def one(j, carry):
            code = codes[source, 0, j]
            ls = lax.rem(lax.shift_right_arithmetic(code, 1), 2)
            rs = lax.rem(code, 2)
            a = jnp.where(ls == 0, block(0), block(1)).reshape(step * height, width)
            x = psi_in[source, :, j].reshape(width, width)
            product = jnp.dot(a, x, preferred_element_type=jnp.float32).astype(jnp.bfloat16)
            wide = jnp.concatenate(
                [product[w * height : (w + 1) * height] for w in range(step)], axis=1
            )
            b = right[rs, pl.ds(c * step, step)].reshape(step * width, width)
            total = jnp.dot(wide, b, preferred_element_type=jnp.float32)
            if c == 0:
                acc[source, j] = total
            else:
                acc[source, j] += total
            return carry

        lax.fori_loop(0, capacity, one, 0, unroll=unroll)

    def sum_copy(source):
        return remote(
            acc.at[source],
            peer.at[lax.rem(source, half)],
            sum_send.at[source],
            sum_recv.at[lax.rem(source, half)],
            {"rep": other},
        )

    def help_sum():
        return remote(
            acc.at[secs], peer.at[half], sum_send.at[secs], sum_recv.at[half], {"rep": other}
        )

    def out_copy():
        return remote(ready, land, out_send, out_recv, {"sec": end})

    def forward_help(c):
        @pl.when(helper)
        def _():
            help_copy(c).wait_recv()
            for h in range(1, rows):
                help_row(c, h, row).start()

    def hand_over(source):
        @pl.when(source // half != rep)
        def _():
            sum_copy(source).start()

    code_copy(me, meta_ref).wait()
    each(lambda at: code_copy(at, meta_far).wait())
    for c in range(chunks):
        work(me, c, lambda s: lenv_ref[s, pl.ds(c * step, step)], rfull)
    hand_over(me)
    each(spread_done)

    for h in range(1, last):
        for c in range(chunks):
            if h == last - 1:
                forward_help(c)

            @pl.when(me >= h)
            def _():
                source = me - h
                l_copy(source, c, lfar.at[source, c], 1).wait_recv()

                @pl.when((me + 1 < secs) & ((me != h) | (me + 1 != last)))
                def _():
                    l_copy(source, c, lfar.at[source, c], 1).start()

            @pl.when(me + h < secs)
            def _():
                source = me + h
                l_copy(source, c, lfar.at[source, c], -1).wait_recv()

                @pl.when((me > 0) & ((me != 1) | (me + h != last)))
                def _():
                    l_copy(source, c, lfar.at[source, c], -1).start()

            @pl.when(me >= h)
            def _():
                source = me - h
                work(source, c, lambda s: lfar[source, c, s], rfull)
                if c == chunks - 1:
                    hand_over(source)

            @pl.when(me + h < secs)
            def _():
                source = me + h
                work(source, c, lambda s: lfar[source, c, s], rfull)
                if c == chunks - 1:
                    hand_over(source)

    @pl.when(helper)
    def _():
        for c in range(chunks):
            for h in range(1, rows):
                help_row(c, h, lax.rem(row + h, rows)).wait_recv()
        for c in range(chunks):
            work(secs, c, lambda s: lfar[opposite, c, s], rhelp)

        @pl.when(lax.div(opposite, half) != rep)
        def _():
            help_sum().start()

        @pl.when(lax.div(opposite, half) == rep)
        def _():
            help_sum().wait_recv()
            for j in range(capacity):
                ready[j] = (acc[secs, j] + peer[half, j]).astype(ready.dtype)
            out_copy().start()

    def finish(i, carry):
        source = rep * half + i

        @pl.when(near(source))
        def _():
            sum_copy(source).wait_recv()
            for j in range(capacity):
                out_ref[i * capacity + j] = (acc[source, j] + peer[i, j]).astype(out_ref.dtype)

        @pl.when(far(source))
        def _():
            out_copy().wait_recv()
            for j in range(capacity):
                out_ref[i * capacity + j] = land[j]

        return carry

    lax.fori_loop(0, half, finish, 0)

    for h in range(1, secs):
        d = lax.rem(me + h, secs)
        meta_copy(d, me).wait_send()
        psi_copy(d, me).wait_send()
    each(spread_left)

    @pl.when(is_end)
    def _():
        for c in range(chunks):
            help_copy(c).wait_send()

    @pl.when(helper)
    def _():
        for c in range(chunks):
            for h in range(1, rows):
                help_row(c, h, row).wait_send()

        @pl.when(lax.div(opposite, half) != rep)
        def _():
            help_sum().wait_send()

        @pl.when(lax.div(opposite, half) == rep)
        def _():
            out_copy().wait_send()

    for h in range(1, rows):
        r_copy(h, row).wait_send()
    for c in range(chunks):
        for h in range(secs):

            @pl.when((me >= h) & (me + 1 < secs) & ((me != h) | (me + 1 != last)))
            def _():
                l_copy(me - h, c, lfar.at[me - h, c], 1).wait_send()

            @pl.when((me + h < secs) & (me > 0) & ((me != 1) | (me + h != last)))
            def _():
                l_copy(me + h, c, lfar.at[me + h, c], -1).wait_send()

    def left(i, carry):
        @pl.when(near(other * half + i))
        def _():
            sum_copy(other * half + i).wait_send()

        return carry

    lax.fori_loop(0, half, left, 0)


def body(rows, psi, left_environment_blocks, right_env, pair_dest, pair_left_sector, pair_right):
    secs = lax.axis_size("sec")
    pairs = psi.shape[0]
    capacity = 2 * pairs // secs
    sectors, bonds, height, width = left_environment_blocks.shape
    chunks = 4
    step = bonds // chunks
    part = width // (2 * rows)
    targets = pair_dest[:, 0]
    places = jnp.arange(pairs)
    same = targets[:, None] == targets[None, :]
    rank = jnp.sum((same & (places[None, :] < places[:, None])).astype(jnp.int32), axis=-1)
    value = (places + 1) * 4 + pair_left_sector * 2 + pair_right
    match = (targets[None, :] == jnp.arange(secs)[:, None])[:, None, :] & (
        rank[None, :] == jnp.arange(128)[:, None]
    )[None]
    meta = jnp.sum(jnp.where(match, value, 0), axis=-1)[:, None, :]
    bf16, f32 = jnp.bfloat16, jnp.float32
    dma = pltpu.SemaphoreType.DMA
    vmem = pl.BlockSpec(memory_space=pltpu.VMEM)
    smem = pl.BlockSpec(memory_space=pltpu.SMEM)
    out = pl.pallas_call(
        functools.partial(kernel, (secs, rows, capacity, chunks)),
        out_shape=jax.ShapeDtypeStruct((capacity * secs // 2, height, width), bf16),
        in_specs=[smem, vmem, vmem, vmem, vmem],
        out_specs=vmem,
        scratch_shapes=[
            pltpu.VMEM((secs + 1, 1, 128), jnp.int32),
            pltpu.SMEM((secs + 1, 1, 128), jnp.int32),
            pltpu.VMEM((secs, capacity, part, width), bf16),
            pltpu.VMEM((secs + 1, 2 * rows, capacity, part, width), bf16),
            pltpu.VMEM((secs, chunks, sectors, step, height, width), bf16),
            pltpu.VMEM((sectors, bonds, rows * height, width), bf16),
            pltpu.VMEM((secs + 1, capacity, height, width), f32),
            pltpu.VMEM((secs // 2 + 1, capacity, height, width), f32),
            pltpu.VMEM((sectors, bonds, rows * height, width), bf16),
            pltpu.VMEM((capacity, height, width), bf16),
            pltpu.VMEM((capacity, height, width), bf16),
            dma((chunks,)),
            dma((chunks,)),
            dma((chunks, rows)),
            dma((chunks, rows)),
            dma,
            dma,
            dma((secs,)),
            dma((secs + 1,)),
            dma((secs + 1,)),
            dma((secs,)),
            dma((secs + 1,)),
            dma((secs + 1, rows)),
            dma((secs + 1, rows)),
            dma((secs + 1, rows)),
            dma((secs + 1, rows)),
            dma((rows,)),
            dma((rows,)),
            dma((secs, chunks)),
            dma((secs, chunks)),
            dma((secs, chunks)),
            dma((secs + 1,)),
            dma((secs // 2 + 1,)),
        ],
        compiler_params=pltpu.CompilerParams(
            collective_id=0, has_side_effects=True, vmem_limit_bytes=56 * 1024 * 1024
        ),
        cost_estimate=pl.CostEstimate(
            flops=4 * secs * capacity * bonds * height * width * width,
            bytes_accessed=8 * 1024 * 1024,
            transcendentals=0,
        ),
    )(meta, meta, psi, left_environment_blocks, right_env)
    return out[None]


def solution(mesh):
    placed = (
        P(("groups", "sec"), None, None),
        P(("groups", "sec"), "rep", "row", None),
        P(("groups", "sec"), "rep", "row", None),
        P(("groups", "sec"), None),
        P(("groups", "sec")),
        P(("groups", "sec")),
    )
    return jax.shard_map(
        functools.partial(body, mesh.shape["row"]),
        mesh=mesh,
        in_specs=placed,
        out_specs=P(("groups", "sec"), "rep", "row", None),
        check_vma=False,
    )
```

```python
import functools

import jax
import jax.numpy as jnp
from jax import lax
from jax.experimental import pallas as pl
from jax.experimental.pallas import tpu as pltpu
from jax.sharding import PartitionSpec as P

MESH = pl.DeviceIdType.MESH


def remote(src, dst, send, recv, where):
    return pltpu.make_async_remote_copy(
        src_ref=src, dst_ref=dst, send_sem=send, recv_sem=recv, device_id=where, device_id_type=MESH
    )


def kernel(
    sizes,
    fill_ref,
    meta_ref,
    psi_ref,
    lenv_ref,
    renv_ref,
    out_ref,
    meta_far,
    codes,
    stage,
    psi_in,
    lfar,
    rfull,
    acc,
    peer,
    rhelp,
    ready,
    land,
    rh_send,
    rh_recv,
    rhrow_send,
    rhrow_recv,
    out_send,
    out_recv,
    meta_send,
    meta_recv,
    code_sem,
    psi_send,
    psi_recv,
    row_send,
    row_recv,
    rep_send,
    rep_recv,
    rrow_send,
    rrow_recv,
    up_send,
    down_send,
    l_recv,
    sum_send,
    sum_recv,
):
    secs, rows, capacity, chunks = sizes
    bonds, height, width = lenv_ref.shape[1:]
    step = bonds // chunks
    part = width // (2 * rows)
    half = secs // 2
    unroll = 4 if capacity % 4 == 0 else capacity
    me = lax.axis_index("sec")
    row = lax.axis_index("row")
    rep = lax.axis_index("rep")
    other = 1 - rep
    mine = row * 2 + rep
    last = secs - 1
    is_end = (me == 0) | (me == last)
    helper = (me == 1) | (me == last - 1)
    end = lax.div(me - 1, secs - 3) * last
    opposite = last - end
    aide = 1 + lax.div(me, last) * (secs - 3)

    def near(a):
        return (me + a != last) | ((me != 0) & (me != last))

    def far(a):
        return (me + a == last) & is_end

    def bars(q):
        return pl.ds(pl.multiple_of(q * part, part), part)

    barrier = pltpu.get_barrier_semaphore()
    for h in range(1, secs):
        pl.semaphore_signal(
            barrier, inc=1, device_id={"sec": lax.rem(me + h, secs)}, device_id_type=MESH
        )
    for h in range(1, rows):
        pl.semaphore_signal(
            barrier, inc=1, device_id={"row": lax.rem(row + h, rows)}, device_id_type=MESH
        )
    pl.semaphore_signal(barrier, inc=1, device_id={"rep": other}, device_id_type=MESH)
    pl.semaphore_wait(barrier, secs + rows - 1)

    def l_copy(source, c, src, direction):
        sends = up_send if direction == 1 else down_send
        return remote(
            src,
            lfar.at[source, c],
            sends.at[source, c],
            l_recv.at[source, c],
            {"sec": me + direction},
        )

    def chunk_of(c):
        return lenv_ref.at[:, pl.ds(c * step, step)]

    def strip(owner):
        return pl.ds(pl.multiple_of(owner * height, height), height)

    def help_copy(c):
        return remote(
            renv_ref.at[:, pl.ds(c * step, step)],
            rhelp.at[:, pl.ds(c * step, step), strip(row)],
            rh_send.at[c],
            rh_recv.at[c],
            {"sec": aide},
        )

    def help_row(c, h, owner):
        block = rhelp.at[:, pl.ds(c * step, step), strip(owner)]
        return remote(
            block,
            block,
            rhrow_send.at[c, h],
            rhrow_recv.at[c, owner],
            {"row": lax.rem(row + h, rows)},
        )

    def fill(d):
        for j in range(capacity):
            p = lax.shift_right_arithmetic(fill_ref[d, 0, j], 2) - 1
            block = psi_ref[jnp.maximum(p, 0), bars(mine), :]
            stage[d, j] = jnp.where(p >= 0, block, jnp.zeros_like(block))

    def psi_copy(d, source):
        return remote(
            stage.at[d],
            psi_in.at[source, mine],
            psi_send.at[d],
            psi_recv.at[source],
            {"sec": d},
        )

    def meta_copy(d, source):
        return remote(
            meta_ref.at[d],
            meta_far.at[source],
            meta_send.at[d],
            meta_recv.at[source],
            {"sec": d},
        )

    def code_copy(source, src):
        return pltpu.make_async_copy(src.at[source], codes.at[source], code_sem.at[source])

    for h in range(1, secs):
        d = lax.rem(me + h, secs)
        fill(d)

        @pl.when(near(d))
        def _():
            meta_copy(d, me).start()
            psi_copy(d, me).start()

        @pl.when(far(d))
        def _():
            to = 1 + lax.div(d, last) * (secs - 3)
            remote(
                meta_ref.at[d], meta_far.at[secs], meta_send.at[d], meta_recv.at[secs], {"sec": to}
            ).start()
            remote(
                stage.at[d],
                psi_in.at[secs, mine],
                psi_send.at[d],
                psi_recv.at[secs],
                {"sec": to},
            ).start()

    code_copy(me, meta_ref).start()

    for c in range(chunks):

        @pl.when(me + 1 < secs)
        def _():
            l_copy(me, c, chunk_of(c), 1).start()

        @pl.when(me > 0)
        def _():
            l_copy(me, c, chunk_of(c), -1).start()

        @pl.when(is_end)
        def _():
            help_copy(c).start()

    def r_copy(h, owner):
        return remote(
            renv_ref,
            rfull.at[:, :, strip(owner)],
            rrow_send.at[h],
            rrow_recv.at[owner],
            {"row": lax.rem(row + h, rows)},
        )

    for h in range(1, rows):
        r_copy(h, row).start()
    rfull[:, :, strip(row)] = renv_ref[...]

    for j in range(capacity):
        p = lax.shift_right_arithmetic(fill_ref[me, 0, j], 2) - 1
        for q in range(2 * rows):
            block = psi_ref[jnp.maximum(p, 0), pl.ds(q * part, part), :]
            psi_in[me, q, j] = jnp.where(p >= 0, block, jnp.zeros_like(block))

    def row_copy(source, h, to):
        return remote(
            psi_in.at[source, mine],
            psi_in.at[source, mine],
            row_send.at[source, h],
            row_recv.at[source, row],
            {"row": to},
        )

    def rep_copy(source, r):
        bar = r * 2 + rep
        return remote(
            psi_in.at[source, bar],
            psi_in.at[source, bar],
            rep_send.at[source, r],
            rep_recv.at[source, r],
            {"rep": other},
        )

    def arrived(source, at):
        meta_copy(me, at).wait_recv()
        code_copy(at, meta_far).start()
        psi_copy(me, at).wait_recv()
        for k in range(1, rows):
            row_copy(at, k, lax.rem(row + k, rows)).start()
        rep_copy(at, row).start()

    def spread(at):
        for k in range(1, rows):
            owner = lax.rem(row + k, rows)
            bar = owner * 2 + rep
            remote(
                psi_in.at[at, bar],
                psi_in.at[at, bar],
                row_send.at[at, k],
                row_recv.at[at, owner],
                {"row": owner},
            ).wait_recv()
            rep_copy(at, owner).start()

    def spread_done(at):
        for r in range(rows):
            rep_copy(at, r).wait_recv()

    def spread_left(at):
        for k in range(1, rows):
            row_copy(at, k, lax.rem(row + k, rows)).wait_send()
        for r in range(rows):
            rep_copy(at, r).wait_send()

    def each(action):
        for h in range(1, secs):
            source = lax.rem(me + secs - h, secs)

            @pl.when(near(source))
            def _():
                action(source)

        @pl.when(helper)
        def _():
            action(secs)

    each(lambda at: arrived(at, at))
    for h in range(1, rows):
        r_copy(h, lax.rem(row + h, rows)).wait_recv()
    each(spread)

    def work(source, c, block, right):
        def one(j, carry):
            code = codes[source, 0, j]
            ls = lax.rem(lax.shift_right_arithmetic(code, 1), 2)
            rs = lax.rem(code, 2)
            a = jnp.where(ls == 0, block(0), block(1)).reshape(step * height, width)
            x = psi_in[source, :, j].reshape(width, width)
            product = jnp.dot(a, x, preferred_element_type=jnp.float32).astype(jnp.bfloat16)
            wide = jnp.concatenate(
                [product[w * height : (w + 1) * height] for w in range(step)], axis=1
            )
            b = right(rs).reshape(step * width, width)
            total = jnp.dot(wide, b, preferred_element_type=jnp.float32)
            if c == 0:
                acc[source, j] = total
            else:
                acc[source, j] += total
            return carry

        lax.fori_loop(0, capacity, one, 0, unroll=unroll)

    def sum_copy(source):
        return remote(
            acc.at[source],
            peer.at[lax.rem(source, half)],
            sum_send.at[source],
            sum_recv.at[lax.rem(source, half)],
            {"rep": other},
        )

    def help_sum():
        return remote(
            acc.at[secs], peer.at[half], sum_send.at[secs], sum_recv.at[half], {"rep": other}
        )

    def out_copy():
        return remote(ready, land, out_send, out_recv, {"sec": end})

    def forward_help(c):
        @pl.when(helper)
        def _():
            help_copy(c).wait_recv()
            for h in range(1, rows):
                help_row(c, h, row).start()

    def help_work(c):
        for h in range(1, rows):
            help_row(c, h, lax.rem(row + h, rows)).wait_recv()

        def chosen(i):
            low, high = (rhelp[n, pl.ds(c * step, step)] for n in range(2))
            return jnp.where(i == 0, low, high)

        work(secs, c, lambda s: lfar[opposite, c, s], chosen)

    def hand_over(source):
        @pl.when(source // half != rep)
        def _():
            sum_copy(source).start()

    code_copy(me, meta_ref).wait()
    each(lambda at: code_copy(at, meta_far).wait())
    for c in range(chunks):
        work(me, c, lambda s: lenv_ref[s, pl.ds(c * step, step)], lambda i: rfull[i, pl.ds(c * step, step)])
    hand_over(me)
    each(spread_done)

    for h in range(1, last):
        for c in range(chunks):
            if h == last - 1:
                forward_help(c)

            @pl.when(me >= h)
            def _():
                source = me - h
                l_copy(source, c, lfar.at[source, c], 1).wait_recv()

                @pl.when((me + 1 < secs) & ((me != h) | (me + 1 != last)))
                def _():
                    l_copy(source, c, lfar.at[source, c], 1).start()

            @pl.when(me + h < secs)
            def _():
                source = me + h
                l_copy(source, c, lfar.at[source, c], -1).wait_recv()

                @pl.when((me > 0) & ((me != 1) | (me + h != last)))
                def _():
                    l_copy(source, c, lfar.at[source, c], -1).start()

            @pl.when(me >= h)
            def _():
                source = me - h
                work(source, c, lambda s: lfar[source, c, s], lambda i: rfull[i, pl.ds(c * step, step)])
                if c == chunks - 1:
                    hand_over(source)

            @pl.when(me + h < secs)
            def _():
                source = me + h
                work(source, c, lambda s: lfar[source, c, s], lambda i: rfull[i, pl.ds(c * step, step)])
                if c == chunks - 1:
                    hand_over(source)

            if h == last - 1 and c > 0:

                @pl.when(helper)
                def _():
                    help_work(c - 1)

    @pl.when(helper)
    def _():
        help_work(chunks - 1)

        @pl.when(lax.div(opposite, half) != rep)
        def _():
            help_sum().start()

        @pl.when(lax.div(opposite, half) == rep)
        def _():
            help_sum().wait_recv()
            for j in range(capacity):
                ready[j] = (acc[secs, j] + peer[half, j]).astype(ready.dtype)
            out_copy().start()

    def finish(i, carry):
        source = rep * half + i

        @pl.when(near(source))
        def _():
            sum_copy(source).wait_recv()
            for j in range(capacity):
                out_ref[i * capacity + j] = (acc[source, j] + peer[i, j]).astype(out_ref.dtype)

        @pl.when(far(source))
        def _():
            out_copy().wait_recv()
            for j in range(capacity):
                out_ref[i * capacity + j] = land[j]

        return carry

    lax.fori_loop(0, half, finish, 0)

    for h in range(1, secs):
        d = lax.rem(me + h, secs)
        meta_copy(d, me).wait_send()
        psi_copy(d, me).wait_send()
    each(spread_left)

    @pl.when(is_end)
    def _():
        for c in range(chunks):
            help_copy(c).wait_send()

    @pl.when(helper)
    def _():
        for c in range(chunks):
            for h in range(1, rows):
                help_row(c, h, row).wait_send()

        @pl.when(lax.div(opposite, half) != rep)
        def _():
            help_sum().wait_send()

        @pl.when(lax.div(opposite, half) == rep)
        def _():
            out_copy().wait_send()

    for h in range(1, rows):
        r_copy(h, row).wait_send()
    for c in range(chunks):
        for h in range(secs):

            @pl.when((me >= h) & (me + 1 < secs) & ((me != h) | (me + 1 != last)))
            def _():
                l_copy(me - h, c, lfar.at[me - h, c], 1).wait_send()

            @pl.when((me + h < secs) & (me > 0) & ((me != 1) | (me + h != last)))
            def _():
                l_copy(me + h, c, lfar.at[me + h, c], -1).wait_send()

    def left(i, carry):
        @pl.when(near(other * half + i))
        def _():
            sum_copy(other * half + i).wait_send()

        return carry

    lax.fori_loop(0, half, left, 0)


def body(rows, psi, left_environment_blocks, right_env, pair_dest, pair_left_sector, pair_right):
    secs = lax.axis_size("sec")
    pairs = psi.shape[0]
    capacity = 2 * pairs // secs
    sectors, bonds, height, width = left_environment_blocks.shape
    chunks = 4
    step = bonds // chunks
    part = width // (2 * rows)
    targets = pair_dest[:, 0]
    places = jnp.arange(pairs)
    same = targets[:, None] == targets[None, :]
    rank = jnp.sum((same & (places[None, :] < places[:, None])).astype(jnp.int32), axis=-1)
    value = (places + 1) * 4 + pair_left_sector * 2 + pair_right
    match = (targets[None, :] == jnp.arange(secs)[:, None])[:, None, :] & (
        rank[None, :] == jnp.arange(128)[:, None]
    )[None]
    meta = jnp.sum(jnp.where(match, value, 0), axis=-1)[:, None, :]
    bf16, f32 = jnp.bfloat16, jnp.float32
    dma = pltpu.SemaphoreType.DMA
    vmem = pl.BlockSpec(memory_space=pltpu.VMEM)
    smem = pl.BlockSpec(memory_space=pltpu.SMEM)
    out = pl.pallas_call(
        functools.partial(kernel, (secs, rows, capacity, chunks)),
        out_shape=jax.ShapeDtypeStruct((capacity * secs // 2, height, width), bf16),
        in_specs=[smem, vmem, vmem, vmem, vmem],
        out_specs=vmem,
        scratch_shapes=[
            pltpu.VMEM((secs + 1, 1, 128), jnp.int32),
            pltpu.SMEM((secs + 1, 1, 128), jnp.int32),
            pltpu.VMEM((secs, capacity, part, width), bf16),
            pltpu.VMEM((secs + 1, 2 * rows, capacity, part, width), bf16),
            pltpu.VMEM((secs, chunks, sectors, step, height, width), bf16),
            pltpu.VMEM((sectors, bonds, rows * height, width), bf16),
            pltpu.VMEM((secs + 1, capacity, height, width), f32),
            pltpu.VMEM((secs // 2 + 1, capacity, height, width), f32),
            pltpu.VMEM((sectors, bonds, rows * height, width), bf16),
            pltpu.VMEM((capacity, height, width), bf16),
            pltpu.VMEM((capacity, height, width), bf16),
            dma((chunks,)),
            dma((chunks,)),
            dma((chunks, rows)),
            dma((chunks, rows)),
            dma,
            dma,
            dma((secs,)),
            dma((secs + 1,)),
            dma((secs + 1,)),
            dma((secs,)),
            dma((secs + 1,)),
            dma((secs + 1, rows)),
            dma((secs + 1, rows)),
            dma((secs + 1, rows)),
            dma((secs + 1, rows)),
            dma((rows,)),
            dma((rows,)),
            dma((secs, chunks)),
            dma((secs, chunks)),
            dma((secs, chunks)),
            dma((secs + 1,)),
            dma((secs // 2 + 1,)),
        ],
        compiler_params=pltpu.CompilerParams(
            collective_id=0, has_side_effects=True, vmem_limit_bytes=56 * 1024 * 1024
        ),
        cost_estimate=pl.CostEstimate(
            flops=4 * secs * capacity * bonds * height * width * width,
            bytes_accessed=8 * 1024 * 1024,
            transcendentals=0,
        ),
    )(meta, meta, psi, left_environment_blocks, right_env)
    return out[None]


def solution(mesh):
    placed = (
        P(("groups", "sec"), None, None),
        P(("groups", "sec"), "rep", "row", None),
        P(("groups", "sec"), "rep", "row", None),
        P(("groups", "sec"), None),
        P(("groups", "sec")),
        P(("groups", "sec")),
    )
    return jax.shard_map(
        functools.partial(body, mesh.shape["row"]),
        mesh=mesh,
        in_specs=placed,
        out_specs=P(("groups", "sec"), "rep", "row", None),
        check_vma=False,
    )
```
